256 devices in a mesh: section: 16 (over x_lo, y, core), dp: 16 (over x_hi, z).
Axes of the slice: x: 4 (x_hi: 2, x_lo: 2; x = x_hi * 2 + x_lo), y: 4, z: 8, core: 2. Of those that a mesh axis runs over, the one named last changes fastest.
Arguments:
- activations: bfloat16 [16, 16, 256, 4096], P('section', 'dp'), may hold values from -6 to 6
- gains: float32 [2, 16, 4096], P(None, 'section'), may hold values from 0.1 to 1.9
- kv_weight: bfloat16 [2, 16, 4096, 1024], P(None, 'section', 'dp'), as said below
- lengths: int32 [16, 16], P('section', 'dp'), may hold values from 64 to 256
Outputs:
- advanced: bfloat16 [16, 16, 256, 4096], P('section', 'dp')
The draws below stay inside these ranges and needn't reach their ends.
Inputs may be any that keep to these rules, and one draw needn't show every extreme that they name: `kv_weight`: projection weights of order one to eight over square root of 4096.
All inputs are finite; a program needn't handle non-finite values.
Results may differ from the reference program's by a relative error of at most 0.022.
Values may be sent and summed in bfloat16 or wider, within the bound.
A program may use at most 128 MiB of HBM per device.

```python
import math
import jax
import jax.numpy as jnp
from jax import lax

HEAD_DIM = 128
REPEATS = 2
TICKS = 3
SEQ = 256
D = 4096
KVW = 512
SECTIONS = 16
N_SECTION = 16
N_DP = 16


def draw_kv_weight(key, part):
    shape = (REPEATS, SECTIONS, D, 2 * KVW)
    base = jax.random.normal(key, shape, jnp.float32) / math.sqrt(D)
    return base.astype(jnp.bfloat16)


def place_ends(array, stream_key, low, largest):
    shape = array.shape
    spot = [jax.random.randint(jax.random.fold_in(stream_key, axis), (), 0, shape[axis]) for axis in range(len(shape))]
    array = array.at[tuple(spot)].set(low)
    longest = shape.index(max(shape))
    spot[longest] = (spot[longest] + 1) % shape[longest]
    return array.at[tuple(spot)].set(largest)


def steps_of(key, shape, split, smallest, largest):
    level, own = 1.0, jax.random.fold_in(key, 6)
    for axis_at, shards_of in split:
        draws = jnp.exp(jax.random.uniform(jax.random.fold_in(own, axis_at), (shards_of,), jnp.float32, smallest / len(split), largest / len(split)))
        level = level * jnp.repeat(draws, shape[axis_at] // shards_of).reshape([-1 if axis == axis_at else 1 for axis in range(len(shape))])
    return level


def gaussian(rng, dims, scale, bound, pieces=(), kind=jnp.bfloat16):
    values = jax.random.normal(rng, dims, jnp.float32) * scale
    if len(pieces) > 0:
        values = steps_of(rng, dims, pieces, -0.22, 0.18) * values
    return jnp.clip(values, min=-bound, max=bound).astype(kind)


def setup_inputs(seed: int = 0) -> dict:
    splits = jax.random.split(jax.random.key(seed), 5)
    return {
        "activations": gaussian(splits[0], (N_SECTION, N_DP, SEQ, D), 1.0, 6.0, ((0, 16), (1, 16))),
        "gains": jnp.clip(1.0 + 0.18 * jax.random.normal(splits[1], (REPEATS, N_SECTION, D), jnp.float32), 0.1, 1.9),
        "kv_weight": draw_kv_weight(jax.random.fold_in(splits[4], 71), 0),
        "lengths": place_ends(jax.random.randint(splits[3], (N_SECTION, N_DP), SEQ // 4, SEQ + 1), jax.random.fold_in(splits[3], 1), SEQ // 4, SEQ).astype(jnp.int32),
    }


def attend(block, gain, weights, length):
    seq = block.shape[0]
    width = weights.shape[1] // 2
    groups = width // HEAD_DIM
    xf = block.astype(jnp.float32)
    factor = lax.rsqrt(lax.optimization_barrier(jnp.mean(xf * xf, axis=-1, keepdims=True)) + 1e-05)
    normed = (xf * factor * gain).astype(jnp.bfloat16)
    keyval = jnp.dot(normed, weights, preferred_element_type=jnp.float32).astype(jnp.bfloat16)
    keys = keyval[:, :width].reshape(seq, groups, HEAD_DIM)
    values = keyval[:, width:].reshape(seq, groups, HEAD_DIM)
    query = normed.reshape(seq, groups, -1, HEAD_DIM)
    scores = jnp.einsum('qhgd,khd->hgqk', query.astype(jnp.float32), keys.astype(jnp.float32)) * HEAD_DIM ** (-0.5)
    places = jnp.arange(seq, dtype=jnp.int32)
    allowed = (places[None, :] <= places[:, None]) & (places[None, :] < length)
    scores = jnp.where(allowed, scores, -1e+30)
    topmost = lax.optimization_barrier(jnp.max(scores, axis=-1, keepdims=True))
    expo = jnp.exp(scores - topmost)
    probs = (expo / lax.optimization_barrier(jnp.sum(expo, axis=-1, keepdims=True))).astype(jnp.bfloat16)
    mixed = jnp.einsum('hgqk,khd->qhgd', probs.astype(jnp.float32), values.astype(jnp.float32)).reshape(seq, -1)
    return (xf + mixed).astype(jnp.bfloat16)

def reference(activations, gains, kv_weight, lengths):
    sections = activations.shape[0]
    groups = activations.shape[1]
    flat = activations.reshape(sections * groups, activations.shape[2], activations.shape[3])
    lens = lengths.reshape(sections * groups)
    for tick in range(TICKS):

        def one_block(index, flat=flat, lens=lens, tick=tick):
            section = index // groups
            repeat = (section < tick).astype(jnp.int32)
            return attend(flat[index], gains[repeat, section], kv_weight[repeat, section], lens[index])
        flat = lax.map(one_block, jnp.arange(sections * groups, dtype=jnp.int32))
        flat = jnp.roll(flat, groups, axis=0)
        lens = jnp.roll(lens, groups, axis=0)
    return flat.reshape(activations.shape)
```

```python
import functools
import math

import jax
import jax.numpy as jnp
from jax import lax
from jax.experimental import pallas as pl
from jax.experimental.pallas import tpu as pltpu
from jax.sharding import PartitionSpec as P

HEAD_DIM = 128
TICKS = 3
RING = 8
KV_HEADS = 4
PER_KV = 8
MESH = pl.DeviceIdType.MESH
SCALE2 = HEAD_DIM ** (-0.5) * math.log2(math.e)


def kernel(
    x_hbm, gains_hbm, w_hbm, len_ref, out_hbm,
    wbuf, stage, xbuf, nbuf, gbuf, lbuf, lown, bias, kbuf, vbuf,
    stage_sem, ring_send, ring_recv, seed_send, x_send, x_recv,
    g_send, g_recv, l_send, l_recv, out_sem,
):
    sections = lax.axis_size("section")
    sec = lax.axis_index("section")
    dp = lax.axis_index("dp")
    z = lax.rem(dp, RING)
    base = dp - z
    seq = xbuf.shape[2]
    cols = xbuf.shape[3]
    rows = stage.shape[2]
    nxt = lax.rem(sec + 1, sections)
    prv = lax.rem(sec + sections - 1, sections)
    across = RING - base + z
    up = base + lax.rem(z + 1, RING)
    down = base + lax.rem(z + RING - 1, RING)
    gives_second = sec <= 1
    has_second = (sec == 1) | (sec == 2)

    def stage_copy(r, h, part):
        return pltpu.make_async_copy(
            w_hbm.at[r, 0, :, pl.ds(part * KV_HEADS * HEAD_DIM + h * HEAD_DIM, HEAD_DIM)],
            stage.at[r, h, :, pl.ds(part * HEAD_DIM, HEAD_DIM)],
            stage_sem.at[r, h, part],
        )

    for h in range(KV_HEADS):
        for part in range(2):
            stage_copy(0, h, part).start()

    @pl.when(gives_second)
    def _():
        for h in range(KV_HEADS):
            for part in range(2):
                stage_copy(1, h, part).start()

    lown[...] = jnp.full(lown.shape, len_ref[0, 0], jnp.int32)

    barrier = pltpu.get_barrier_semaphore()
    for peer in ((nxt, dp), (nxt, across), (prv, dp), (prv, across), (sec, up), (sec, down)):
        pl.semaphore_signal(barrier, inc=1, device_id=peer, device_id_type=MESH)
    pl.semaphore_wait(barrier, 6)

    def block(ref, r, h, blk):
        return ref.at[r, h, pl.ds(pl.multiple_of(blk * rows, rows), rows), :]

    def seed(r, h, side):
        return pltpu.make_async_remote_copy(
            src_ref=stage.at[r, h],
            dst_ref=block(wbuf, r, h, dp),
            send_sem=seed_send.at[r, h, side],
            recv_sem=ring_recv.at[r, h, dp],
            device_id=(nxt, across if side else dp),
            device_id_type=MESH,
        )

    def ring(r, h, half, k, way):
        blk = half * RING + lax.rem(z + (k if way else RING - k), RING)
        return pltpu.make_async_remote_copy(
            src_ref=block(wbuf, r, h, blk),
            dst_ref=block(wbuf, r, h, blk),
            send_sem=ring_send.at[r, way, h, half, k],
            recv_sem=ring_recv.at[r, h, blk],
            device_id=(sec, down if way else up),
            device_id_type=MESH,
        )

    def step(r, group, k):
        def one(q, carry):
            h = group * 2 + q // 2
            half = lax.rem(q, 2)
            if k == 0:
                ring(r, h, half, 0, 0).wait_recv()
                ring(r, h, half, 0, 0).start()
                ring(r, h, half, 0, 1).start()
            elif k < 3:
                ring(r, h, half, k, 0).wait_recv()
                ring(r, h, half, k, 0).start()
                ring(r, h, half, k, 1).wait_recv()
                ring(r, h, half, k, 1).start()
            elif k == 3:
                ring(r, h, half, k, 0).wait_recv()

                @pl.when(lax.rem(h, 2) == 0)
                def _():
                    ring(r, h, half, k, 0).start()

                ring(r, h, half, k, 1).wait_recv()

                @pl.when(lax.rem(h, 2) == 1)
                def _():
                    ring(r, h, half, k, 1).start()
            else:
                ring(r, h, half, k, 0).wait_recv()
            return carry

        lax.fori_loop(0, 4, one, 0)

    def ring_done(r):
        def one(q, carry):
            h = q // 2
            half = lax.rem(q, 2)
            for k in range(3):
                ring(r, h, half, k, 0).wait_send()
                ring(r, h, half, k, 1).wait_send()

            @pl.when(lax.rem(h, 2) == 0)
            def _():
                ring(r, h, half, 3, 0).wait_send()

            @pl.when(lax.rem(h, 2) == 1)
            def _():
                ring(r, h, half, 3, 1).wait_send()

            return carry

        lax.fori_loop(0, 2 * KV_HEADS, one, 0)

    def first_x(c):
        return pltpu.make_async_remote_copy(
            src_ref=x_hbm.at[0, 0, :, pl.ds(c * cols, cols)],
            dst_ref=xbuf.at[0, c],
            send_sem=x_send.at[0, c],
            recv_sem=x_recv.at[0, c],
            device_id=(nxt, dp),
            device_id_type=MESH,
        )

    def shift_x(t, c):
        return pltpu.make_async_remote_copy(
            src_ref=xbuf.at[jnp.maximum(t - 1, 0), c],
            dst_ref=xbuf.at[t, c],
            send_sem=x_send.at[t, c],
            recv_sem=x_recv.at[t, c],
            device_id=(nxt, dp),
            device_id_type=MESH,
        )

    def shift_len(t, src):
        return pltpu.make_async_remote_copy(
            src_ref=src,
            dst_ref=lbuf.at[t],
            send_sem=l_send.at[t],
            recv_sem=l_recv.at[t],
            device_id=(nxt, dp),
            device_id_type=MESH,
        )

    move_gains = pltpu.make_async_remote_copy(
        src_ref=gains_hbm, dst_ref=gbuf, send_sem=g_send, recv_sem=g_recv,
        device_id=(nxt, dp), device_id_type=MESH,
    )

    def write(c):
        return pltpu.make_async_copy(
            xbuf.at[TICKS - 1, c],
            out_hbm.at[0, 0, :, pl.ds(pl.multiple_of(c * cols, cols), cols)],
            out_sem.at[c],
        )

    for h in range(KV_HEADS):
        for part in range(2):
            stage_copy(0, h, part).wait()
        seed(0, h, 0).start()
        seed(0, h, 1).start()
    move_gains.start()
    shift_len(0, lown).start()
    for c in range(KV_HEADS):
        first_x(c).start()

    @pl.when(gives_second)
    def _():
        for h in range(KV_HEADS):
            for part in range(2):
                stage_copy(1, h, part).wait()
            seed(1, h, 0).start()
            seed(1, h, 1).start()

    vbuf[:, HEAD_DIM:] = jnp.ones((seq, HEAD_DIM), jnp.bfloat16)

    step(0, 0, 0)
    step(0, 0, 1)
    step(0, 0, 2)
    step(0, 1, 0)
    step(0, 0, 3)
    move_gains.wait_recv()

    def one_head(i, carry):
        t = i // KV_HEADS
        h = lax.rem(i, KV_HEADS)
        r = ((sec >= 1) & (t >= sec)).astype(jnp.int32)

        @pl.when(i == 1)
        def _():
            step(0, 1, 2)

        @pl.when(i == 2)
        def _():
            step(0, 1, 3)

            @pl.when(has_second)
            def _():
                step(1, 0, 0)
                step(1, 1, 0)

            step(0, 1, 4)

        @pl.when((i == KV_HEADS) & has_second)
        def _():
            step(1, 0, 1)
            step(1, 1, 1)

        @pl.when(((i == KV_HEADS) & (sec == 1)) | ((i == 2 * KV_HEADS) & (sec == 2)))
        def _():
            for k in range(2, 5):
                step(1, 0, k)
                step(1, 1, k)

        @pl.when(h == 0)
        def _():
            shift_len(t, lown).wait_recv()

            @pl.when(t < TICKS - 1)
            def _():
                shift_len(t + 1, lbuf.at[t]).start()

            for c in range(KV_HEADS):
                shift_x(t, c).wait_recv()

            places = lax.broadcasted_iota(jnp.int32, (seq, seq), 0)
            keys = lax.broadcasted_iota(jnp.int32, (seq, seq), 1)
            allowed = (keys <= places) & (keys < lbuf[t][0:1, :])
            bias[...] = jnp.where(allowed, 0.0, -1e30)

            def norm_rows(b, carry):
                at = pl.ds(pl.multiple_of(b * 32, 32), 32)
                total = jnp.zeros((32, HEAD_DIM), jnp.float32)
                for c in range(KV_HEADS):
                    xf = xbuf[t, c, at, :].astype(jnp.float32)
                    sq = xf * xf
                    for g in range(cols // HEAD_DIM):
                        total = total + sq[:, g * HEAD_DIM:(g + 1) * HEAD_DIM]
                mean = jnp.sum(total, axis=-1, keepdims=True) / (cols * KV_HEADS)
                factor = lax.rsqrt(mean + 1e-05)
                for c in range(KV_HEADS):
                    xf = xbuf[t, c, at, :].astype(jnp.float32)
                    gain = gbuf[r, 0:1, c * cols:(c + 1) * cols]
                    nbuf[at, c * cols:(c + 1) * cols] = (xf * factor * gain).astype(jnp.bfloat16)
                return carry

            lax.fori_loop(0, seq // 32, norm_rows, 0)

        @pl.when(i == 0)
        def _():
            step(0, 0, 4)
            step(0, 1, 1)

        keyval = jnp.dot(nbuf[...], wbuf[r, h], preferred_element_type=jnp.float32)
        kbuf[...] = keyval[:, :HEAD_DIM].astype(jnp.bfloat16)
        vbuf[:, :HEAD_DIM] = keyval[:, HEAD_DIM:].astype(jnp.bfloat16)

        def heads(pair, carry):
            for jj in range(4):
                j = pair * 4 + jj
                at = pl.ds(pl.multiple_of(h * cols + j * HEAD_DIM, HEAD_DIM), HEAD_DIM)
                put = pl.ds(pl.multiple_of(j * HEAD_DIM, HEAD_DIM), HEAD_DIM)
                for half in range(2):
                    mine = slice(half * seq // 2, (half + 1) * seq // 2)
                    seen = (half + 1) * seq // 2
                    scores = lax.dot_general(
                        nbuf[mine, at], kbuf[:seen, :], (((1,), (1,)), ((), ())),
                        preferred_element_type=jnp.float32,
                    ) + bias[mine, :seen]
                    top = jnp.max(scores, axis=-1, keepdims=True)
                    expo = jnp.exp2((scores - top) * SCALE2).astype(jnp.bfloat16)
                    both = jnp.dot(expo, vbuf[:seen, :], preferred_element_type=jnp.float32)
                    mixed = both[:, :HEAD_DIM] / both[:, HEAD_DIM:]
                    old = xbuf[t, h, mine, put].astype(jnp.float32)
                    xbuf[t, h, mine, put] = (old + mixed).astype(jnp.bfloat16)
            return carry

        lax.fori_loop(0, PER_KV // 4, heads, 0)

        @pl.when(t < TICKS - 1)
        def _():
            shift_x(t + 1, h).start()

        @pl.when(t == TICKS - 1)
        def _():
            write(h).start()

        return carry

    lax.fori_loop(0, TICKS * KV_HEADS, one_head, 0)

    move_gains.wait_send()
    for t in range(TICKS):
        shift_len(t, lown).wait_send()
    for c in range(KV_HEADS):
        first_x(c).wait_send()
        shift_x(1, c).wait_send()
        shift_x(2, c).wait_send()
    for h in range(KV_HEADS):
        seed(0, h, 0).wait_send()
        seed(0, h, 1).wait_send()
    ring_done(0)

    @pl.when(gives_second)
    def _():
        for h in range(KV_HEADS):
            seed(1, h, 0).wait_send()
            seed(1, h, 1).wait_send()

    @pl.when(has_second)
    def _():
        ring_done(1)

    for c in range(KV_HEADS):
        write(c).wait()


def per_device(activations, gains, kv_weight, lengths):
    seq, width = activations.shape[2:]
    rows = kv_weight.shape[2]
    blocks = lax.axis_size("dp")
    cols = width // KV_HEADS
    dma = pltpu.SemaphoreType.DMA
    return pl.pallas_call(
        kernel,
        out_shape=jax.ShapeDtypeStruct(activations.shape, activations.dtype),
        in_specs=[
            pl.BlockSpec(memory_space=pl.ANY),
            pl.BlockSpec(memory_space=pl.ANY),
            pl.BlockSpec(memory_space=pl.ANY),
            pl.BlockSpec(memory_space=pltpu.SMEM),
        ],
        out_specs=pl.BlockSpec(memory_space=pl.ANY),
        scratch_shapes=[
            pltpu.VMEM((2, KV_HEADS, blocks * rows, 2 * HEAD_DIM), jnp.bfloat16),
            pltpu.VMEM((2, KV_HEADS, rows, 2 * HEAD_DIM), jnp.bfloat16),
            pltpu.VMEM((TICKS, KV_HEADS, seq, cols), jnp.bfloat16),
            pltpu.VMEM((seq, width), jnp.bfloat16),
            pltpu.VMEM(gains.shape, jnp.float32),
            pltpu.VMEM((TICKS, 8, seq), jnp.int32),
            pltpu.VMEM((8, seq), jnp.int32),
            pltpu.VMEM((seq, seq), jnp.float32),
            pltpu.VMEM((seq, HEAD_DIM), jnp.bfloat16),
            pltpu.VMEM((seq, 2 * HEAD_DIM), jnp.bfloat16),
            dma((2, KV_HEADS, 2)),
            dma((2, 2, KV_HEADS, 2, 5)),
            dma((2, KV_HEADS, blocks)),
            dma((2, KV_HEADS, 2)),
            dma((TICKS, KV_HEADS)),
            dma((TICKS, KV_HEADS)),
            dma, dma,
            dma((TICKS,)),
            dma((TICKS,)),
            dma((KV_HEADS,)),
        ],
        compiler_params=pltpu.CompilerParams(
            collective_id=0, has_side_effects=True, vmem_limit_bytes=56 * 1024 * 1024
        ),
        name="relay",
    )(activations, gains, kv_weight, lengths)


def solution(mesh):
    return jax.shard_map(
        per_device,
        mesh=mesh,
        in_specs=(
            P("section", "dp", None, None),
            P(None, "section", None),
            P(None, "section", "dp", None),
            P("section", "dp"),
        ),
        out_specs=P("section", "dp", None, None),
        check_vma=False,
    )
```

```python
import functools
import math

import jax
import jax.numpy as jnp
from jax import lax
from jax.experimental import pallas as pl
from jax.experimental.pallas import tpu as pltpu
from jax.sharding import PartitionSpec as P

HEAD_DIM = 128
TICKS = 3
RING = 8
KV_HEADS = 4
PER_KV = 8
MESH = pl.DeviceIdType.MESH
SCALE2 = HEAD_DIM ** (-0.5) * math.log2(math.e)


def kernel(
    x_hbm, gains_hbm, w_hbm, len_ref, out_hbm,
    wbuf, stage, xbuf, nbuf, gbuf, lbuf, lown, bias, kbuf, vbuf,
    stage_sem, ring_send, ring_recv, seed_send, cross_send, x_send, x_recv,
    g_send, g_recv, l_send, l_recv, out_sem,
):
    sections = lax.axis_size("section")
    sec = lax.axis_index("section")
    dp = lax.axis_index("dp")
    z = lax.rem(dp, RING)
    base = dp - z
    seq = xbuf.shape[2]
    cols = xbuf.shape[3]
    rows = stage.shape[2]
    nxt = lax.rem(sec + 1, sections)
    prv = lax.rem(sec + sections - 1, sections)
    here = base // RING
    there = 1 - here
    across = there * RING + z
    up = base + lax.rem(z + 1, RING)
    down = base + lax.rem(z + RING - 1, RING)
    gives_second = sec <= 1
    has_second = (sec == 1) | (sec == 2)
    direct = jnp.where(lax.rem(sec, 8) >= 6, 1, 2)

    def stage_copy(r, h, part):
        return pltpu.make_async_copy(
            w_hbm.at[r, 0, :, pl.ds(part * KV_HEADS * HEAD_DIM + h * HEAD_DIM, HEAD_DIM)],
            stage.at[r, h, :, pl.ds(part * HEAD_DIM, HEAD_DIM)],
            stage_sem.at[r, h, part],
        )

    for h in range(KV_HEADS):
        for part in range(2):
            stage_copy(0, h, part).start()

    @pl.when(gives_second)
    def _():
        for h in range(KV_HEADS):
            for part in range(2):
                stage_copy(1, h, part).start()

    lown[...] = jnp.full(lown.shape, len_ref[0, 0], jnp.int32)

    barrier = pltpu.get_barrier_semaphore()
    for peer in ((nxt, dp), (prv, dp), (sec, across), (sec, up), (sec, down)):
        pl.semaphore_signal(barrier, inc=1, device_id=peer, device_id_type=MESH)
    pl.semaphore_wait(barrier, 5)

    def block(ref, r, h, blk):
        return ref.at[r, h, pl.ds(pl.multiple_of(blk * rows, rows), rows), :]

    def seed(r, h):
        return pltpu.make_async_remote_copy(
            src_ref=stage.at[r, h],
            dst_ref=block(wbuf, r, h, dp),
            send_sem=seed_send.at[r, h],
            recv_sem=ring_recv.at[r, h, dp],
            device_id=(nxt, dp),
            device_id_type=MESH,
        )

    def cross(r, h, half, k, way):
        blk = half * RING + lax.rem(z + (k if way else RING - k), RING)
        return pltpu.make_async_remote_copy(
            src_ref=block(wbuf, r, h, blk),
            dst_ref=block(wbuf, r, h, blk),
            send_sem=cross_send.at[r, way, h, k],
            recv_sem=ring_recv.at[r, h, blk],
            device_id=(sec, across),
            device_id_type=MESH,
        )

    def ring(r, h, half, k, way):
        blk = half * RING + lax.rem(z + (k if way else RING - k), RING)
        return pltpu.make_async_remote_copy(
            src_ref=block(wbuf, r, h, blk),
            dst_ref=block(wbuf, r, h, blk),
            send_sem=ring_send.at[r, way, h, half, k],
            recv_sem=ring_recv.at[r, h, blk],
            device_id=(sec, down if way else up),
            device_id_type=MESH,
        )

    def step_a(r, k):
        def one(h, carry):
            if k == 0:
                ring(r, h, here, 0, 0).wait_recv()
                ring(r, h, here, 0, 0).start()
                ring(r, h, here, 0, 1).start()
                cross(r, h, here, 0, 0).start()
            elif k < 4:
                for way in range(2):
                    ring(r, h, here, k, way).wait_recv()
                    if k < 3:
                        ring(r, h, here, k, way).start()
                    else:

                        @pl.when(h == way)
                        def _():
                            ring(r, h, here, k, way).start()

                    cross(r, h, here, k, way).start()
            else:
                ring(r, h, here, k, 0).wait_recv()
                cross(r, h, here, k, 0).start()
            return carry

        lax.fori_loop(0, direct, one, 0)

    def landed(r, h):
        ring(r, h, there, 0, 0).wait_recv()
        for k in range(1, 4):
            ring(r, h, there, k, 0).wait_recv()
            ring(r, h, there, k, 1).wait_recv()
        ring(r, h, there, 4, 0).wait_recv()

    def cross_b(r):
        def one(h, carry):
            ring(r, h, here, 0, 0).wait_recv()
            cross(r, h, here, 0, 0).start()
            return carry

        lax.fori_loop(direct, KV_HEADS, one, 0)

    def step_b(r, h, k):
        def one(second, carry):
            half = jnp.where(second == 0, here, there)
            if k == 0:

                @pl.when(second == 1)
                def _():
                    ring(r, h, half, 0, 0).wait_recv()

                ring(r, h, half, 0, 0).start()
                ring(r, h, half, 0, 1).start()
            elif k < 4:
                for way in range(2):
                    ring(r, h, half, k, way).wait_recv()
                    if k < 3:
                        ring(r, h, half, k, way).start()
                    else:

                        @pl.when(lax.rem(h + second, 2) == way)
                        def _():
                            ring(r, h, half, k, way).start()

            else:
                ring(r, h, half, k, 0).wait_recv()
            return carry

        lax.fori_loop(0, 2, one, 0)

    def slot(r, n):
        for m in range(KV_HEADS - 1):
            if 0 <= n - 2 * m <= 4:

                @pl.when(direct + m < KV_HEADS)
                def _():
                    step_b(r, direct + m, n - 2 * m)

    def pair(r, k):
        step_b(r, 2, k)
        step_b(r, 3, k)

    def ring_sent(r, h, half, last):
        for k in range(3):
            ring(r, h, half, k, 0).wait_send()
            ring(r, h, half, k, 1).wait_send()

        @pl.when(last == 0)
        def _():
            ring(r, h, half, 3, 0).wait_send()

        @pl.when(last == 1)
        def _():
            ring(r, h, half, 3, 1).wait_send()

    def all_sent(r):
        def one_a(h, carry):
            ring_sent(r, h, here, lax.rem(h, 2))
            for k in range(5):
                cross(r, h, here, k, 0).wait_send()
            for k in range(1, 4):
                cross(r, h, here, k, 1).wait_send()
            return carry

        def one_b(h, carry):
            ring_sent(r, h, here, lax.rem(h, 2))
            ring_sent(r, h, there, lax.rem(h + 1, 2))
            cross(r, h, here, 0, 0).wait_send()
            return carry

        lax.fori_loop(0, direct, one_a, 0)
        lax.fori_loop(direct, KV_HEADS, one_b, 0)

    def first_x(c):
        return pltpu.make_async_remote_copy(
            src_ref=x_hbm.at[0, 0, :, pl.ds(c * cols, cols)],
            dst_ref=xbuf.at[0, c],
            send_sem=x_send.at[0, c],
            recv_sem=x_recv.at[0, c],
            device_id=(nxt, dp),
            device_id_type=MESH,
        )

    def shift_x(t, c):
        return pltpu.make_async_remote_copy(
            src_ref=xbuf.at[jnp.maximum(t - 1, 0), c],
            dst_ref=xbuf.at[t, c],
            send_sem=x_send.at[t, c],
            recv_sem=x_recv.at[t, c],
            device_id=(nxt, dp),
            device_id_type=MESH,
        )

    def shift_len(t, src):
        return pltpu.make_async_remote_copy(
            src_ref=src,
            dst_ref=lbuf.at[t],
            send_sem=l_send.at[t],
            recv_sem=l_recv.at[t],
            device_id=(nxt, dp),
            device_id_type=MESH,
        )

    move_gains = pltpu.make_async_remote_copy(
        src_ref=gains_hbm, dst_ref=gbuf, send_sem=g_send, recv_sem=g_recv,
        device_id=(nxt, dp), device_id_type=MESH,
    )

    def write(c):
        return pltpu.make_async_copy(
            xbuf.at[TICKS - 1, c],
            out_hbm.at[0, 0, :, pl.ds(pl.multiple_of(c * cols, cols), cols)],
            out_sem.at[c],
        )

    def seeds(r, heads):
        for h in heads:
            for part in range(2):
                stage_copy(r, h, part).wait()
            seed(r, h).start()

    vbuf[:, HEAD_DIM:] = jnp.ones((seq, HEAD_DIM), jnp.bfloat16)

    seeds(0, (0, 1))
    step_a(0, 0)
    for h in (0, 1):
        seed(0, h).wait_send()
    seeds(0, (2, 3))
    cross_b(0)
    for h in (2, 3):
        seed(0, h).wait_send()
    move_gains.start()
    shift_len(0, lown).start()
    for c in range(KV_HEADS):
        first_x(c).start()

    @pl.when(gives_second)
    def _():
        seeds(1, range(KV_HEADS))

    step_a(0, 1)
    step_a(0, 2)
    slot(0, 0)
    step_a(0, 3)
    step_a(0, 4)
    slot(0, 1)
    move_gains.wait_recv()

    def one_head(i, carry):
        t = i // KV_HEADS
        h = lax.rem(i, KV_HEADS)
        r = ((sec >= 1) & (t >= sec)).astype(jnp.int32)

        def both(first, second):
            return ((sec == 1) & (i == first)) | ((sec == 2) & (i == second))

        @pl.when(i == 1)
        def _():
            slot(0, 5)

        @pl.when(i == direct + 1)
        def _():
            slot(0, 6)

        @pl.when(i == 3)
        def _():
            slot(0, 7)
            slot(0, 8)

        @pl.when((i == 2) & has_second)
        def _():
            step_a(1, 0)
            cross_b(1)

        @pl.when((i == 3) & has_second)
        def _():
            step_a(1, 1)

        @pl.when((i == 4) & has_second)
        def _():
            step_a(1, 2)
            pair(1, 0)

        @pl.when(both(4, 4))
        def _():
            step_a(1, 3)
            step_a(1, 4)

        @pl.when(both(4, 5))
        def _():
            pair(1, 1)

        @pl.when(h == 0)
        def _():
            shift_len(t, lown).wait_recv()

            @pl.when(t < TICKS - 1)
            def _():
                shift_len(t + 1, lbuf.at[t]).start()

            for c in range(KV_HEADS):
                shift_x(t, c).wait_recv()

            places = lax.broadcasted_iota(jnp.int32, (seq, seq), 0)
            keys = lax.broadcasted_iota(jnp.int32, (seq, seq), 1)
            allowed = (keys <= places) & (keys < lbuf[t][0:1, :])
            bias[...] = jnp.where(allowed, 0.0, -1e30)

            def norm_rows(b, carry):
                at = pl.ds(pl.multiple_of(b * 32, 32), 32)
                total = jnp.zeros((32, HEAD_DIM), jnp.float32)
                for c in range(KV_HEADS):
                    xf = xbuf[t, c, at, :].astype(jnp.float32)
                    sq = xf * xf
                    for g in range(cols // HEAD_DIM):
                        total = total + sq[:, g * HEAD_DIM:(g + 1) * HEAD_DIM]
                mean = jnp.sum(total, axis=-1, keepdims=True) / (cols * KV_HEADS)
                factor = lax.rsqrt(mean + 1e-05)
                for c in range(KV_HEADS):
                    xf = xbuf[t, c, at, :].astype(jnp.float32)
                    gain = gbuf[r, 0:1, c * cols:(c + 1) * cols]
                    nbuf[at, c * cols:(c + 1) * cols] = (xf * factor * gain).astype(jnp.bfloat16)
                return carry

            lax.fori_loop(0, seq // 32, norm_rows, 0)

        @pl.when(i == 0)
        def _():
            slot(0, 2)
            slot(0, 3)
            slot(0, 4)

        @pl.when(both(4, 6))
        def _():
            pair(1, 2)

        @pl.when(both(5, 7))
        def _():
            pair(1, 3)

        @pl.when(both(6, 10))
        def _():
            pair(1, 4)

        @pl.when((h < direct) & ((t == 0) | (t == sec)))
        def _():
            landed(r, h)

        keyval = jnp.dot(nbuf[...], wbuf[r, h], preferred_element_type=jnp.float32)
        kbuf[...] = keyval[:, :HEAD_DIM].astype(jnp.bfloat16)
        vbuf[:, :HEAD_DIM] = keyval[:, HEAD_DIM:].astype(jnp.bfloat16)

        def heads(part, carry):
            for jj in range(4):
                j = part * 4 + jj
                at = pl.ds(pl.multiple_of(h * cols + j * HEAD_DIM, HEAD_DIM), HEAD_DIM)
                put = pl.ds(pl.multiple_of(j * HEAD_DIM, HEAD_DIM), HEAD_DIM)
                for half in range(2):
                    mine = slice(half * seq // 2, (half + 1) * seq // 2)
                    seen = (half + 1) * seq // 2
                    scores = lax.dot_general(
                        nbuf[mine, at], kbuf[:seen, :], (((1,), (1,)), ((), ())),
                        preferred_element_type=jnp.float32,
                    ) + bias[mine, :seen]
                    top = jnp.max(scores, axis=-1, keepdims=True)
                    expo = jnp.exp2((scores - top) * SCALE2).astype(jnp.bfloat16)
                    both = jnp.dot(expo, vbuf[:seen, :], preferred_element_type=jnp.float32)
                    mixed = both[:, :HEAD_DIM] / both[:, HEAD_DIM:]
                    old = xbuf[t, h, mine, put].astype(jnp.float32)
                    xbuf[t, h, mine, put] = (old + mixed).astype(jnp.bfloat16)
            return carry

        lax.fori_loop(0, PER_KV // 4, heads, 0)

        @pl.when(t < TICKS - 1)
        def _():
            shift_x(t + 1, h).start()

        @pl.when(t == TICKS - 1)
        def _():
            write(h).start()

        return carry

    lax.fori_loop(0, TICKS * KV_HEADS, one_head, 0)

    move_gains.wait_send()
    for t in range(TICKS):
        shift_len(t, lown).wait_send()
    for c in range(KV_HEADS):
        first_x(c).wait_send()
        shift_x(1, c).wait_send()
        shift_x(2, c).wait_send()
    all_sent(0)

    @pl.when(gives_second)
    def _():
        for h in range(KV_HEADS):
            seed(1, h).wait_send()

    @pl.when(has_second)
    def _():
        all_sent(1)

    for c in range(KV_HEADS):
        write(c).wait()


def per_device(activations, gains, kv_weight, lengths):
    seq, width = activations.shape[2:]
    rows = kv_weight.shape[2]
    blocks = lax.axis_size("dp")
    cols = width // KV_HEADS
    dma = pltpu.SemaphoreType.DMA
    return pl.pallas_call(
        kernel,
        out_shape=jax.ShapeDtypeStruct(activations.shape, activations.dtype),
        in_specs=[
            pl.BlockSpec(memory_space=pl.ANY),
            pl.BlockSpec(memory_space=pl.ANY),
            pl.BlockSpec(memory_space=pl.ANY),
            pl.BlockSpec(memory_space=pltpu.SMEM),
        ],
        out_specs=pl.BlockSpec(memory_space=pl.ANY),
        scratch_shapes=[
            pltpu.VMEM((2, KV_HEADS, blocks * rows, 2 * HEAD_DIM), jnp.bfloat16),
            pltpu.VMEM((2, KV_HEADS, rows, 2 * HEAD_DIM), jnp.bfloat16),
            pltpu.VMEM((TICKS, KV_HEADS, seq, cols), jnp.bfloat16),
            pltpu.VMEM((seq, width), jnp.bfloat16),
            pltpu.VMEM(gains.shape, jnp.float32),
            pltpu.VMEM((TICKS, 8, seq), jnp.int32),
            pltpu.VMEM((8, seq), jnp.int32),
            pltpu.VMEM((seq, seq), jnp.float32),
            pltpu.VMEM((seq, HEAD_DIM), jnp.bfloat16),
            pltpu.VMEM((seq, 2 * HEAD_DIM), jnp.bfloat16),
            dma((2, KV_HEADS, 2)),
            dma((2, 2, KV_HEADS, 2, 5)),
            dma((2, KV_HEADS, blocks)),
            dma((2, KV_HEADS)),
            dma((2, 2, KV_HEADS, 5)),
            dma((TICKS, KV_HEADS)),
            dma((TICKS, KV_HEADS)),
            dma, dma,
            dma((TICKS,)),
            dma((TICKS,)),
            dma((KV_HEADS,)),
        ],
        compiler_params=pltpu.CompilerParams(
            collective_id=0, has_side_effects=True, vmem_limit_bytes=56 * 1024 * 1024
        ),
        name="relay",
    )(activations, gains, kv_weight, lengths)


def solution(mesh):
    return jax.shard_map(
        per_device,
        mesh=mesh,
        in_specs=(
            P("section", "dp", None, None),
            P(None, "section", None),
            P(None, "section", "dp", None),
            P("section", "dp"),
        ),
        out_specs=P("section", "dp", None, None),
        check_vma=False,
    )
```

```python
import functools
import math

import jax
import jax.numpy as jnp
from jax import lax
from jax.experimental import pallas as pl
from jax.experimental.pallas import tpu as pltpu
from jax.sharding import PartitionSpec as P

HEAD_DIM = 128
TICKS = 3
RING = 8
KV_HEADS = 4
PER_KV = 8
MESH = pl.DeviceIdType.MESH
SCALE2 = HEAD_DIM ** (-0.5) * math.log2(math.e)


def kernel(
    x_hbm, gains_hbm, w_hbm, len_ref, out_hbm,
    wbuf, stage, xbuf, nbuf, gbuf, lbuf, lown, bias, kbuf, vbuf,
    stage_sem, ring_send, ring_recv, seed_send, cross_send, x_send, x_recv,
    g_send, g_recv, l_send, l_recv, out_sem,
):
    sections = lax.axis_size("section")
    sec = lax.axis_index("section")
    dp = lax.axis_index("dp")
    z = lax.rem(dp, RING)
    base = dp - z
    seq = xbuf.shape[2]
    cols = xbuf.shape[3]
    rows = stage.shape[2]
    nxt = lax.rem(sec + 1, sections)
    prv = lax.rem(sec + sections - 1, sections)
    here = base // RING
    there = 1 - here
    across = there * RING + z
    up = base + lax.rem(z + 1, RING)
    down = base + lax.rem(z + RING - 1, RING)
    gives_second = sec <= 1
    has_second = (sec == 1) | (sec == 2)
    direct = jnp.where(lax.rem(sec, 8) >= 6, 1, 2)

    def stage_copy(r, h, part):
        return pltpu.make_async_copy(
            w_hbm.at[r, 0, :, pl.ds(part * KV_HEADS * HEAD_DIM + h * HEAD_DIM, HEAD_DIM)],
            stage.at[r, h, :, pl.ds(part * HEAD_DIM, HEAD_DIM)],
            stage_sem.at[r, h, part],
        )

    for h in range(KV_HEADS):
        for part in range(2):
            stage_copy(0, h, part).start()

    @pl.when(gives_second)
    def _():
        for h in range(KV_HEADS):
            for part in range(2):
                stage_copy(1, h, part).start()

    lown[...] = jnp.full(lown.shape, len_ref[0, 0], jnp.int32)

    barrier = pltpu.get_barrier_semaphore()
    for peer in ((nxt, dp), (prv, dp), (sec, across), (sec, up), (sec, down)):
        pl.semaphore_signal(barrier, inc=1, device_id=peer, device_id_type=MESH)
    pl.semaphore_wait(barrier, 5)

    def block(ref, r, h, blk):
        return ref.at[r, h, pl.ds(pl.multiple_of(blk * rows, rows), rows), :]

    def seed(r, h):
        return pltpu.make_async_remote_copy(
            src_ref=stage.at[r, h],
            dst_ref=block(wbuf, r, h, dp),
            send_sem=seed_send.at[r, h],
            recv_sem=ring_recv.at[r, h, dp],
            device_id=(nxt, dp),
            device_id_type=MESH,
        )

    def cross(r, h, half, k, way):
        blk = half * RING + lax.rem(z + (k if way else RING - k), RING)
        return pltpu.make_async_remote_copy(
            src_ref=block(wbuf, r, h, blk),
            dst_ref=block(wbuf, r, h, blk),
            send_sem=cross_send.at[r, way, h, k],
            recv_sem=ring_recv.at[r, h, blk],
            device_id=(sec, across),
            device_id_type=MESH,
        )

    def ring(r, h, half, k, way):
        blk = half * RING + lax.rem(z + (k if way else RING - k), RING)
        return pltpu.make_async_remote_copy(
            src_ref=block(wbuf, r, h, blk),
            dst_ref=block(wbuf, r, h, blk),
            send_sem=ring_send.at[r, way, h, half, k],
            recv_sem=ring_recv.at[r, h, blk],
            device_id=(sec, down if way else up),
            device_id_type=MESH,
        )

    def step_a(r, k):
        def one(h, carry):
            if k == 0:
                ring(r, h, here, 0, 0).wait_recv()
                ring(r, h, here, 0, 0).start()
                ring(r, h, here, 0, 1).start()
                cross(r, h, here, 0, 0).start()
            elif k < 4:
                for way in range(2):
                    ring(r, h, here, k, way).wait_recv()
                    if k < 3:
                        ring(r, h, here, k, way).start()
                    else:

                        @pl.when(h == way)
                        def _():
                            ring(r, h, here, k, way).start()

                    cross(r, h, here, k, way).start()
            else:
                ring(r, h, here, k, 0).wait_recv()
                cross(r, h, here, k, 0).start()
            return carry

        lax.fori_loop(0, direct, one, 0)

    def landed(r, h):
        ring(r, h, there, 0, 0).wait_recv()
        for k in range(1, 4):
            ring(r, h, there, k, 0).wait_recv()
            ring(r, h, there, k, 1).wait_recv()
        ring(r, h, there, 4, 0).wait_recv()

    def cross_b(r):
        def one(h, carry):
            ring(r, h, here, 0, 0).wait_recv()
            cross(r, h, here, 0, 0).start()
            return carry

        lax.fori_loop(direct, KV_HEADS, one, 0)

    def step_b(r, h, k):
        def one(second, carry):
            half = jnp.where(second == 0, here, there)
            if k == 0:

                @pl.when(second == 1)
                def _():
                    ring(r, h, half, 0, 0).wait_recv()

                ring(r, h, half, 0, 0).start()
                ring(r, h, half, 0, 1).start()
            elif k < 4:
                for way in range(2):
                    ring(r, h, half, k, way).wait_recv()
                    if k < 3:
                        ring(r, h, half, k, way).start()
                    else:

                        @pl.when(lax.rem(h + second, 2) == way)
                        def _():
                            ring(r, h, half, k, way).start()

            else:
                ring(r, h, half, k, 0).wait_recv()
            return carry

        lax.fori_loop(0, 2, one, 0)

    def slot(r, n):
        for m in range(KV_HEADS - 1):
            if 0 <= n - 2 * m <= 4:

                @pl.when(direct + m < KV_HEADS)
                def _():
                    step_b(r, direct + m, n - 2 * m)

    def pair(r, k):
        step_b(r, 2, k)
        step_b(r, 3, k)

    def ring_sent(r, h, half, last):
        for k in range(3):
            ring(r, h, half, k, 0).wait_send()
            ring(r, h, half, k, 1).wait_send()

        @pl.when(last == 0)
        def _():
            ring(r, h, half, 3, 0).wait_send()

        @pl.when(last == 1)
        def _():
            ring(r, h, half, 3, 1).wait_send()

    def all_sent(r):
        def one_a(h, carry):
            ring_sent(r, h, here, lax.rem(h, 2))
            for k in range(5):
                cross(r, h, here, k, 0).wait_send()
            for k in range(1, 4):
                cross(r, h, here, k, 1).wait_send()
            return carry

        def one_b(h, carry):
            ring_sent(r, h, here, lax.rem(h, 2))
            ring_sent(r, h, there, lax.rem(h + 1, 2))
            cross(r, h, here, 0, 0).wait_send()
            return carry

        lax.fori_loop(0, direct, one_a, 0)
        lax.fori_loop(direct, KV_HEADS, one_b, 0)

    def first_x(c):
        return pltpu.make_async_remote_copy(
            src_ref=x_hbm.at[0, 0, :, pl.ds(c * cols, cols)],
            dst_ref=xbuf.at[0, c],
            send_sem=x_send.at[0, c],
            recv_sem=x_recv.at[0, c],
            device_id=(nxt, dp),
            device_id_type=MESH,
        )

    def shift_x(t, c):
        return pltpu.make_async_remote_copy(
            src_ref=xbuf.at[jnp.maximum(t - 1, 0), c],
            dst_ref=xbuf.at[t, c],
            send_sem=x_send.at[t, c],
            recv_sem=x_recv.at[t, c],
            device_id=(nxt, dp),
            device_id_type=MESH,
        )

    def shift_len(t, src):
        return pltpu.make_async_remote_copy(
            src_ref=src,
            dst_ref=lbuf.at[t],
            send_sem=l_send.at[t],
            recv_sem=l_recv.at[t],
            device_id=(nxt, dp),
            device_id_type=MESH,
        )

    move_gains = pltpu.make_async_remote_copy(
        src_ref=gains_hbm, dst_ref=gbuf, send_sem=g_send, recv_sem=g_recv,
        device_id=(nxt, dp), device_id_type=MESH,
    )

    def write(c):
        return pltpu.make_async_copy(
            xbuf.at[TICKS - 1, c],
            out_hbm.at[0, 0, :, pl.ds(pl.multiple_of(c * cols, cols), cols)],
            out_sem.at[c],
        )

    def seeds(r, heads):
        for h in heads:
            for part in range(2):
                stage_copy(r, h, part).wait()
            seed(r, h).start()

    vbuf[:, HEAD_DIM:] = jnp.ones((seq, HEAD_DIM), jnp.bfloat16)

    seeds(0, (0, 1))
    step_a(0, 0)
    for h in (0, 1):
        seed(0, h).wait_send()
    seeds(0, (2, 3))
    cross_b(0)
    for h in (2, 3):
        seed(0, h).wait_send()
    move_gains.start()
    shift_len(0, lown).start()
    for c in range(KV_HEADS):
        first_x(c).start()

    @pl.when(gives_second)
    def _():
        seeds(1, range(KV_HEADS))

    step_a(0, 1)
    step_a(0, 2)
    slot(0, 0)
    step_a(0, 3)
    step_a(0, 4)
    slot(0, 1)
    move_gains.wait_recv()

    def one_head(i, carry):
        t = i // KV_HEADS
        h = lax.rem(i, KV_HEADS)
        r = ((sec >= 1) & (t >= sec)).astype(jnp.int32)

        def both(first, second):
            return ((sec == 1) & (i == first)) | ((sec == 2) & (i == second))

        @pl.when(i == 1)
        def _():
            slot(0, 5)

        @pl.when(i == direct + 1)
        def _():
            slot(0, 6)

        @pl.when(i == 3)
        def _():
            slot(0, 7)
            slot(0, 8)

        @pl.when((i == 2) & has_second)
        def _():
            step_a(1, 0)
            cross_b(1)

        @pl.when((i == 3) & has_second)
        def _():
            step_a(1, 1)

        @pl.when((i == 4) & has_second)
        def _():
            step_a(1, 2)
            pair(1, 0)

        @pl.when(both(4, 4))
        def _():
            step_a(1, 3)
            step_a(1, 4)

        @pl.when(both(4, 5))
        def _():
            pair(1, 1)

        @pl.when(h == 0)
        def _():
            shift_len(t, lown).wait_recv()

            @pl.when(t < TICKS - 1)
            def _():
                shift_len(t + 1, lbuf.at[t]).start()

            for c in range(KV_HEADS):
                shift_x(t, c).wait_recv()

            places = lax.broadcasted_iota(jnp.int32, (seq, seq), 0)
            keys = lax.broadcasted_iota(jnp.int32, (seq, seq), 1)
            allowed = (keys <= places) & (keys < lbuf[t][0:1, :])
            bias[...] = jnp.where(allowed, 0.0, -1e30)

            def norm_rows(b, carry):
                at = pl.ds(pl.multiple_of(b * 32, 32), 32)
                total = jnp.zeros((32, HEAD_DIM), jnp.float32)
                for c in range(KV_HEADS):
                    xf = xbuf[t, c, at, :].astype(jnp.float32)
                    sq = xf * xf
                    for g in range(cols // HEAD_DIM):
                        total = total + sq[:, g * HEAD_DIM:(g + 1) * HEAD_DIM]
                mean = jnp.sum(total, axis=-1, keepdims=True) / (cols * KV_HEADS)
                factor = lax.rsqrt(mean + 1e-05)
                for c in range(KV_HEADS):
                    xf = xbuf[t, c, at, :].astype(jnp.float32)
                    gain = gbuf[r, 0:1, c * cols:(c + 1) * cols]
                    nbuf[at, c * cols:(c + 1) * cols] = (xf * factor * gain).astype(jnp.bfloat16)
                return carry

            lax.fori_loop(0, seq // 32, norm_rows, 0)

        @pl.when(i == 0)
        def _():
            slot(0, 2)
            slot(0, 3)
            slot(0, 4)

        @pl.when(both(4, 6))
        def _():
            pair(1, 2)

        @pl.when(both(5, 7))
        def _():
            pair(1, 3)

        @pl.when(both(6, 10))
        def _():
            pair(1, 4)

        @pl.when((h < direct) & ((t == 0) | (t == sec)))
        def _():
            landed(r, h)

        keyval = jnp.dot(nbuf[...], wbuf[r, h], preferred_element_type=jnp.float32)
        kbuf[...] = keyval[:, :HEAD_DIM].astype(jnp.bfloat16)
        vbuf[:, :HEAD_DIM] = keyval[:, HEAD_DIM:].astype(jnp.bfloat16)

        todo = [(jj, half) for jj in range(4) for half in range(2)]

        def span(half):
            return slice(half * seq // 2, (half + 1) * seq // 2), (half + 1) * seq // 2

        def heads(part, carry):
            def place(jj, start):
                at = start + (part * 4 + jj) * HEAD_DIM
                return pl.ds(pl.multiple_of(at, HEAD_DIM), HEAD_DIM)

            scored = []
            for jj, half in todo:
                mine, seen = span(half)
                scored.append(
                    lax.dot_general(
                        nbuf[mine, place(jj, h * cols)], kbuf[:seen, :], (((1,), (1,)), ((), ())),
                        preferred_element_type=jnp.float32,
                    ) + bias[mine, :seen]
                )
            weights = []
            for scores in scored:
                top = jnp.max(scores, axis=-1, keepdims=True)
                weights.append(jnp.exp2((scores - top) * SCALE2).astype(jnp.bfloat16))
            for (jj, half), expo in zip(todo, weights):
                mine, seen = span(half)
                put = place(jj, 0)
                summed = jnp.dot(expo, vbuf[:seen, :], preferred_element_type=jnp.float32)
                mixed = summed[:, :HEAD_DIM] / summed[:, HEAD_DIM:]
                old = xbuf[t, h, mine, put].astype(jnp.float32)
                xbuf[t, h, mine, put] = (old + mixed).astype(jnp.bfloat16)
            return carry

        lax.fori_loop(0, PER_KV // 4, heads, 0)

        @pl.when(t < TICKS - 1)
        def _():
            shift_x(t + 1, h).start()

        @pl.when(t == TICKS - 1)
        def _():
            write(h).start()

        return carry

    lax.fori_loop(0, TICKS * KV_HEADS, one_head, 0)

    move_gains.wait_send()
    for t in range(TICKS):
        shift_len(t, lown).wait_send()
    for c in range(KV_HEADS):
        first_x(c).wait_send()
        shift_x(1, c).wait_send()
        shift_x(2, c).wait_send()
    all_sent(0)

    @pl.when(gives_second)
    def _():
        for h in range(KV_HEADS):
            seed(1, h).wait_send()

    @pl.when(has_second)
    def _():
        all_sent(1)

    for c in range(KV_HEADS):
        write(c).wait()


def per_device(activations, gains, kv_weight, lengths):
    seq, width = activations.shape[2:]
    rows = kv_weight.shape[2]
    blocks = lax.axis_size("dp")
    cols = width // KV_HEADS
    dma = pltpu.SemaphoreType.DMA
    return pl.pallas_call(
        kernel,
        out_shape=jax.ShapeDtypeStruct(activations.shape, activations.dtype),
        in_specs=[
            pl.BlockSpec(memory_space=pl.ANY),
            pl.BlockSpec(memory_space=pl.ANY),
            pl.BlockSpec(memory_space=pl.ANY),
            pl.BlockSpec(memory_space=pltpu.SMEM),
        ],
        out_specs=pl.BlockSpec(memory_space=pl.ANY),
        scratch_shapes=[
            pltpu.VMEM((2, KV_HEADS, blocks * rows, 2 * HEAD_DIM), jnp.bfloat16),
            pltpu.VMEM((2, KV_HEADS, rows, 2 * HEAD_DIM), jnp.bfloat16),
            pltpu.VMEM((TICKS, KV_HEADS, seq, cols), jnp.bfloat16),
            pltpu.VMEM((seq, width), jnp.bfloat16),
            pltpu.VMEM(gains.shape, jnp.float32),
            pltpu.VMEM((TICKS, 8, seq), jnp.int32),
            pltpu.VMEM((8, seq), jnp.int32),
            pltpu.VMEM((seq, seq), jnp.float32),
            pltpu.VMEM((seq, HEAD_DIM), jnp.bfloat16),
            pltpu.VMEM((seq, 2 * HEAD_DIM), jnp.bfloat16),
            dma((2, KV_HEADS, 2)),
            dma((2, 2, KV_HEADS, 2, 5)),
            dma((2, KV_HEADS, blocks)),
            dma((2, KV_HEADS)),
            dma((2, 2, KV_HEADS, 5)),
            dma((TICKS, KV_HEADS)),
            dma((TICKS, KV_HEADS)),
            dma, dma,
            dma((TICKS,)),
            dma((TICKS,)),
            dma((KV_HEADS,)),
        ],
        compiler_params=pltpu.CompilerParams(
            collective_id=0, has_side_effects=True, vmem_limit_bytes=56 * 1024 * 1024
        ),
        name="relay",
    )(activations, gains, kv_weight, lengths)


def solution(mesh):
    return jax.shard_map(
        per_device,
        mesh=mesh,
        in_specs=(
            P("section", "dp", None, None),
            P(None, "section", None),
            P(None, "section", "dp", None),
            P("section", "dp"),
        ),
        out_specs=P("section", "dp", None, None),
        check_vma=False,
    )
```
